32 devices in a mesh: replica: 8 (over y, x, core), tensor: 4 (over z).
Axes of the slice: x: 2, y: 2, z: 4, core: 2. Of those that a mesh axis runs over, the one named last changes fastest.
Arguments:
- attention_heads_output: bfloat16 [2048, 8192], P('replica', 'tensor'), may hold values from -6 to 6
- output_projection_weight: bfloat16 [8192, 8192], P('tensor'), may hold values from -0.0625 to 0.0625
- adapter_down_factors: bfloat16 [512, 64, 8192], P(None, 'replica', 'tensor'), may hold values from -0.0625 to 0.0625
- adapter_up_factors: bfloat16 [512, 64, 8192], P(None, 'replica', 'tensor'), may hold values from -0.75 to 0.75
- group_working_adapters: int32 [8, 8], replicated, may hold values from 0 to 511, as said below
- adapter_store_row: int32 [512], replicated, may hold values from 0 to 511, each once
- request_working_slot: int32 [2048], P('replica'), may hold values from 0 to 7
Outputs:
- projected: bfloat16 [2048, 8192], P('replica', 'tensor')
The draws below stay inside these ranges and needn't reach their ends.
Inputs may be any that keep to these rules, and one draw needn't show every extreme that they name: `group_working_adapters`: the 8 ids of one group are distinct. `adapter_store_row`: each adapter has its own row.
All inputs are finite; a program needn't handle non-finite values.
Results may differ from the reference program's by a relative error of at most 0.0028.
Values may be sent and summed in bfloat16 or wider, within the bound.
A program may use at most 128 MiB of HBM per device.

```python
import math
import jax
import jax.numpy as jnp
import numpy as np
from jax import lax

MODEL_WIDTH = 8192
ADAPTER_RANK = 64
REQ = 256
STORE_ADAPTERS = 512
WORKING_SLOTS = 8
GROUPS = 8
TOKENS = 2048


def draw_group_working_adapters(key, part):
    key = jax.random.fold_in(key, 11)
    keys = jax.random.split(key, GROUPS)

    def single(one_key):
        return jax.random.permutation(one_key, STORE_ADAPTERS)[:WORKING_SLOTS]
    return jax.vmap(single)(keys).astype(jnp.int32)


def set_ends(values, rng, low, top_value):
    place = [jax.random.randint(jax.random.fold_in(rng, axis), (), 0, length) for axis, length in enumerate(values.shape)]
    main_axis = values.shape.index(max(values.shape))
    beside = place[:main_axis] + [(place[main_axis] + 1) % values.shape[main_axis]] + place[main_axis + 1:]
    return values.at[tuple(place)].set(low).at[tuple(beside)].set(top_value)


def block_levels(key, dims, shards, least, top_value):
    factor_of = 1.0
    for dim, blocks in shards:
        draws = jax.random.uniform(jax.random.fold_in(jax.random.fold_in(key, 6), dim), (blocks,), jnp.float32, least / len(shards), top_value / len(shards))
        factor_of = factor_of * jnp.repeat(jnp.exp(draws), dims[dim] // blocks).reshape((-1,) + (1,) * (len(dims) - 1 - dim))
    return factor_of


def rank_bounds(count, slope):
    loads = [(1 << 20) // math.isqrt(standing ** slope) + 1 for standing in range(1, count + 1)]
    deviation = 1 + sum(loads) // (1 << 30)
    return np.cumsum(np.array([max(1, weight // deviation) for weight in loads]))


def skewed_ids(rng, extent, amount, lean):
    table = rank_bounds(amount, lean)
    lot = jax.random.randint(jax.random.fold_in(rng, 1), extent, 0, int(table[amount - 1]))
    rank = jnp.searchsorted(jnp.asarray(table, jnp.int32), lot, side="right")
    return jax.random.permutation(jax.random.fold_in(rng, 2), amount)[rank].astype(jnp.int32)


def bell_draw(own_key, dims, deviation, reach, shards=(), kind=jnp.bfloat16):
    entries = jax.random.normal(own_key, dims, jnp.float32) * deviation
    if len(shards) > 0:
        entries = block_levels(own_key, dims, shards, -0.22, 0.18) * entries
    return jnp.clip(entries, min=-reach, max=reach).astype(kind)


def setup_inputs(seed: int = 0) -> dict:
    seeds = jax.random.split(jax.random.key(seed), 8)
    return {
        "attention_heads_output": bell_draw(seeds[0], (TOKENS, MODEL_WIDTH), 1.0, 6.0, ((0, 8), (1, 4))),
        "output_projection_weight": bell_draw(seeds[1], (MODEL_WIDTH, MODEL_WIDTH), MODEL_WIDTH ** -0.5, 0.0625, ((0, 4),)),
        "adapter_down_factors": bell_draw(seeds[2], (STORE_ADAPTERS, ADAPTER_RANK, MODEL_WIDTH), MODEL_WIDTH ** -0.5, 0.0625, ((1, 8), (2, 4))),
        "adapter_up_factors": bell_draw(seeds[3], (STORE_ADAPTERS, ADAPTER_RANK, MODEL_WIDTH), ADAPTER_RANK ** -0.5, 0.75, ((1, 8), (2, 4))),
        "group_working_adapters": draw_group_working_adapters(jax.random.fold_in(seeds[7], 71), 0),
        "adapter_store_row": jax.random.permutation(seeds[5], STORE_ADAPTERS).astype(jnp.int32),
        "request_working_slot": set_ends(skewed_ids(seeds[6], (TOKENS,), WORKING_SLOTS, 2), jax.random.fold_in(seeds[6], 3), 0, WORKING_SLOTS - 1).astype(jnp.int32),
    }


ADAPTER_SCALE = 0.5


def reference(attention_heads_output, output_projection_weight, adapter_down_factors, adapter_up_factors, group_working_adapters, adapter_store_row, request_working_slot):
    def one_group(packed):
        block, slot_ids, adapter_ids = packed
        chosen_adapter_index = jnp.take(adapter_store_row, adapter_ids, axis=0).astype(jnp.int32)
        down_factor_rows = jnp.take(adapter_down_factors, chosen_adapter_index, axis=0).reshape(WORKING_SLOTS * ADAPTER_RANK, MODEL_WIDTH)
        up_factor_rows = jnp.take(adapter_up_factors, chosen_adapter_index, axis=0).reshape(WORKING_SLOTS * ADAPTER_RANK, MODEL_WIDTH)
        selector = (slot_ids[:, None] == jnp.arange(WORKING_SLOTS, dtype=jnp.int32)[None, :]).astype(jnp.float32)
        base_projection = jnp.dot(block, output_projection_weight, preferred_element_type=jnp.float32)
        all_ranks = lax.dot_general(block, down_factor_rows, (((1,), (1,)), ((), ())), preferred_element_type=jnp.float32)
        rank_part = jnp.sum(all_ranks.reshape(REQ, WORKING_SLOTS, ADAPTER_RANK) * selector[:, :, None], axis=1)
        rounded = rank_part.astype(jnp.bfloat16)
        expanded = (rounded[:, None, :] * selector[:, :, None].astype(jnp.bfloat16)).reshape(REQ, WORKING_SLOTS * ADAPTER_RANK)
        adapter_contribution = jnp.dot(expanded, up_factor_rows, preferred_element_type=jnp.float32)
        return (base_projection + ADAPTER_SCALE * adapter_contribution).astype(jnp.bfloat16)

    result = lax.map(one_group, (attention_heads_output.reshape(GROUPS, REQ, MODEL_WIDTH), request_working_slot.reshape(GROUPS, REQ), group_working_adapters))
    return result.reshape(TOKENS, MODEL_WIDTH)
```

```python
import functools

import jax
import jax.numpy as jnp
from jax import lax
from jax.experimental import pallas as pl
from jax.experimental.pallas import tpu as pltpu
from jax.sharding import PartitionSpec as P

ADAPTER_RANK = 64
WORKING_SLOTS = 8


ADAPTER_SCALE = 0.5


def body(
    attention_heads_output,
    output_projection_weight,
    adapter_down_factors,
    adapter_up_factors,
    group_working_adapters,
    adapter_store_row,
    request_working_slot,
):
    groups = lax.axis_size("replica")
    row_count, features = attention_heads_output.shape
    local_rank_count = adapter_down_factors.shape[1]
    needed_store_rows = jnp.take(adapter_store_row, group_working_adapters.reshape(-1), axis=0)
    outgoing_down_factors = jnp.take(adapter_down_factors, needed_store_rows, axis=0)
    outgoing_up_factors = jnp.take(adapter_up_factors, needed_store_rows, axis=0)
    outgoing = jnp.stack([outgoing_down_factors, outgoing_up_factors], axis=1).reshape(
        groups, WORKING_SLOTS, 2, local_rank_count * features
    )
    fetched = lax.all_to_all(outgoing, "replica", split_axis=0, concat_axis=0, tiled=True)
    fetched = fetched.reshape(groups, WORKING_SLOTS, 2, local_rank_count, features).transpose(
        2, 1, 0, 3, 4
    )
    fetched = fetched.reshape(2, WORKING_SLOTS * ADAPTER_RANK, features)
    down_factor_rows = fetched[0]
    up_factor_rows = fetched[1]
    selector = (
        request_working_slot[:, None] == jnp.arange(WORKING_SLOTS, dtype=jnp.int32)[None, :]
    ).astype(jnp.float32)
    all_ranks = lax.dot_general(
        attention_heads_output,
        down_factor_rows,
        (((1,), (1,)), ((), ())),
        preferred_element_type=jnp.float32,
    )
    rank_local = jnp.sum(
        all_ranks.reshape(row_count, WORKING_SLOTS, ADAPTER_RANK) * selector[:, :, None], axis=1
    )
    base_local = jnp.dot(
        attention_heads_output, output_projection_weight, preferred_element_type=jnp.float32
    )
    base_projection_sum = lax.psum_scatter(base_local, "tensor", scatter_dimension=1, tiled=True)
    rank_total = lax.psum(rank_local, "tensor")
    rounded = rank_total.astype(jnp.bfloat16)
    expanded = (rounded[:, None, :] * selector[:, :, None].astype(jnp.bfloat16)).reshape(
        row_count, WORKING_SLOTS * ADAPTER_RANK
    )
    adapter_contribution = jnp.dot(expanded, up_factor_rows, preferred_element_type=jnp.float32)
    return (base_projection_sum + ADAPTER_SCALE * adapter_contribution).astype(jnp.bfloat16)


MESH = pl.DeviceIdType.MESH
ANY = pl.BlockSpec(memory_space=pl.ANY)
VMEM = pl.BlockSpec(memory_space=pltpu.VMEM)
SMEM = pl.BlockSpec(memory_space=pltpu.SMEM)
F32 = jnp.float32
BF16 = jnp.bfloat16

LINE = 4
SUB = 4
BLOCKS = LINE * SUB
SLOTS_W = 4


def gather_kernel(ids, store, down, up, out_down, out_up, sems):
    count = out_down.shape[0]

    def copies(i, row):
        return (
            pltpu.make_async_copy(down.at[row], out_down.at[i], sems.at[0, i]),
            pltpu.make_async_copy(up.at[row], out_up.at[i], sems.at[1, i]),
        )

    def start(i, carry):
        for copy in copies(i, store[ids[i // WORKING_SLOTS, i % WORKING_SLOTS]]):
            copy.start()
        return carry

    def finish(i, carry):
        for copy in copies(i, 0):
            copy.wait()
        return carry

    lax.fori_loop(0, count, start, 0)
    lax.fori_loop(0, count, finish, 0)


def fold_matrix(columns, ranks, half):
    c = lax.broadcasted_iota(jnp.int32, (columns, 2 * ranks), 0)
    t = lax.broadcasted_iota(jnp.int32, (columns, 2 * ranks), 1)
    target = (c // (WORKING_SLOTS * 8)) * 8 + c % 8 + half * ranks
    return jnp.where(target == t, 1.0, 0.0).astype(BF16)


def spread_matrix(columns, ranks, half):
    t = lax.broadcasted_iota(jnp.int32, (2 * ranks, columns), 0)
    c = lax.broadcasted_iota(jnp.int32, (2 * ranks, columns), 1)
    target = (c // (WORKING_SLOTS * 8)) * 8 + c % 8 + half * ranks
    return jnp.where(target == t, 1.0, 0.0).astype(BF16)


def main_kernel(
    groups,
    x_ref, slot_ref, w_ref, down_ref, up_ref, out_ref,
    wbuf, acc, sbuf, from_end, from_mid, from_far, got_down, got_up, term,
    rank_own, rank_end, rank_far, rank_total,
    w_sem, send_sem, end_sem, mid_sem, far_sem, fetch_send, fetch_recv, own_sem, rank_send, rank_recv,
):
    me = lax.axis_index("replica")
    z = lax.axis_index("tensor")
    upper = z // 2
    inner = (z + upper) % 2
    is_end = inner == 0
    is_mid = inner == 1
    beside = 3 * upper + (1 - 2 * upper) * (1 - inner)
    far_mid = 3 * upper + (1 - 2 * upper) * 2
    far_end = 3 * upper + (1 - 2 * upper) * 3

    rows, depth = x_ref.shape
    width = out_ref.shape[1] // SUB
    ranks = ADAPTER_RANK
    fetched = groups * WORKING_SLOTS * 8

    def w_copy(p, slot):
        place = (3 + inner - p // SUB + LINE) % LINE
        chunk = 3 * upper + (1 - 2 * upper) * place
        column = pl.multiple_of((chunk * SUB + p % SUB) * width, width)
        return pltpu.make_async_copy(w_ref.at[:, pl.ds(column, width)], wbuf.at[slot], w_sem.at[slot])

    for p in range(SLOTS_W):
        w_copy(p, p).start()

    barrier = pltpu.get_barrier_semaphore()
    for k in range(1, groups):
        pl.semaphore_signal(barrier, inc=1, device_id=((me + k) % groups, z), device_id_type=MESH)
    for k in range(1, LINE):
        pl.semaphore_signal(barrier, inc=1, device_id=(me, (z + k) % LINE), device_id_type=MESH)
    pl.semaphore_wait(barrier, groups - 1 + LINE - 1)

    def fetch(which, k):
        src, dst = ((down_ref, got_down), (up_ref, got_up))[which]
        to = (me + k) % groups
        return pltpu.make_async_remote_copy(
            src_ref=src.at[to], dst_ref=dst.at[me],
            send_sem=fetch_send.at[which, k], recv_sem=fetch_recv.at[which, k],
            device_id=(to, z), device_id_type=MESH,
        )

    def fetch_own(which):
        src, dst = ((down_ref, got_down), (up_ref, got_up))[which]
        return pltpu.make_async_copy(src.at[me], dst.at[me], own_sem.at[which])

    def fetch_start(which):
        for k in range(1, groups):
            fetch(which, k).start()
        fetch_own(which).start()

    def fetch_wait(which):
        for k in range(1, groups):
            fetch(which, k).wait()
        fetch_own(which).wait()

    def to_beside_mid(p):
        return pltpu.make_async_remote_copy(
            src_ref=sbuf.at[p], dst_ref=from_end.at[p], send_sem=send_sem.at[p], recv_sem=end_sem.at[p],
            device_id=(me, beside), device_id_type=MESH)

    def to_beside_end(p):
        return pltpu.make_async_remote_copy(
            src_ref=sbuf.at[p], dst_ref=from_mid.at[p], send_sem=send_sem.at[p], recv_sem=mid_sem.at[p],
            device_id=(me, beside), device_id_type=MESH)

    def to_far(p, j, device):
        return pltpu.make_async_remote_copy(
            src_ref=sbuf.at[p], dst_ref=from_far.at[j], send_sem=send_sem.at[p], recv_sem=far_sem.at[j],
            device_id=(me, device), device_id_type=MESH)

    fetch_start(0)

    def block(p, carry):
        slot = p % SLOTS_W
        w_copy(p, slot).wait()
        part = jnp.dot(x_ref[...], wbuf[slot], preferred_element_type=F32)
        sent = jnp.where(is_end, p < 3 * SUB, p < SUB)

        @pl.when(sent)
        def _():
            sbuf[p] = part.astype(BF16)

        @pl.when(jnp.logical_not(sent))
        def _():
            acc[p - SUB] = part

        @pl.when(jnp.logical_and(is_end, sent))
        def _():
            to_beside_mid(p).start()

        @pl.when(jnp.logical_and(is_mid, sent))
        def _():
            to_beside_end(p).start()

        @pl.when(p + SLOTS_W < BLOCKS)
        def _():
            w_copy(p + SLOTS_W, slot).start()

        return carry

    lax.fori_loop(0, BLOCKS, block, 0)
    fetch_start(1)

    def merge(p, carry):
        to_beside_mid(p - SUB).wait_recv()
        sbuf[p] = (acc[p - SUB] + from_end[p - SUB].astype(F32)).astype(BF16)
        return carry

    def merge_far_end(j, carry):
        merge(SUB + j, carry)
        to_far(SUB + j, j, far_end).start()
        return carry

    def merge_far_mid(j, carry):
        merge(2 * SUB + j, carry)
        to_far(2 * SUB + j, j, far_mid).start()
        return carry

    fetch_wait(0)
    down_rows = got_down[...].astype(F32).reshape(fetched, depth).astype(BF16)
    every = lax.dot_general(x_ref[...], down_rows, (((1,), (1,)), ((), ())), preferred_element_type=F32)
    column_slot = (lax.broadcasted_iota(jnp.int32, (rows, fetched), 1) // 8) % WORKING_SLOTS
    chosen = slot_ref[...] == column_slot
    every = jnp.where(chosen, every, 0.0)
    half = rows // 2
    total = jnp.zeros((half, 2 * ranks), F32)
    for h in range(2):
        rest = every[h * half:(h + 1) * half]
        matrix = fold_matrix(fetched, ranks, h)
        for _ in range(3):
            piece = rest.astype(BF16)
            total = total + jnp.dot(piece, matrix, preferred_element_type=F32)
            rest = rest - piece.astype(F32)
    rank_own[...] = total

    def rank_copy(i, src, dst, device):
        return pltpu.make_async_remote_copy(
            src_ref=src, dst_ref=dst, send_sem=rank_send.at[i], recv_sem=rank_recv.at[i],
            device_id=(me, device), device_id_type=MESH)

    to_mid = rank_copy(0, rank_own, rank_end, beside)
    across = rank_copy(1, rank_own, rank_far, far_mid)
    to_end = rank_copy(2, rank_own, rank_total, beside)

    @pl.when(is_end)
    def _():
        to_mid.start()

    @pl.when(is_mid)
    def _():
        lax.fori_loop(0, SUB, merge_far_end, 0)
        to_mid.wait_recv()
        rank_own[...] += rank_end[...]
        across.start()
        across.wait_recv()
        across.wait_send()
        rank_own[...] += rank_far[...]
        to_end.start()
        rank_total[...] = rank_own[...]
        lax.fori_loop(0, SUB, merge_far_mid, 0)
        to_end.wait_send()

    @pl.when(is_end)
    def _():
        to_mid.wait_send()
        to_end.wait_recv()

    fetch_wait(1)
    rounded = rank_total[...].astype(BF16)
    parts = [
        jnp.dot(rounded, spread_matrix(fetched, ranks, h), preferred_element_type=F32) for h in range(2)
    ]
    expanded = jnp.where(chosen, jnp.concatenate(parts, axis=0), 0.0).astype(BF16)
    term[...] = got_up[...].astype(F32).reshape(fetched, out_ref.shape[1]).astype(BF16)

    for j in range(SUB):
        columns = slice(j * width, (j + 1) * width)
        adapter = jnp.dot(expanded, term[:, columns], preferred_element_type=F32)
        acc[2 * SUB + j] += ADAPTER_SCALE * adapter

    for j in range(SUB):
        columns = slice(j * width, (j + 1) * width)
        to_far(j, j, far_mid).wait_recv()

        @pl.when(is_end)
        def _():
            to_beside_end(j).wait_recv()
            total = acc[2 * SUB + j] + from_mid[j].astype(F32) + from_far[j].astype(F32)
            out_ref[:, columns] = total.astype(BF16)

        @pl.when(is_mid)
        def _():
            to_beside_mid(2 * SUB + j).wait_recv()
            total = acc[2 * SUB + j] + from_end[2 * SUB + j].astype(F32) + from_far[j].astype(F32)
            out_ref[:, columns] = total.astype(BF16)

    def drain(p, carry):
        to_beside_mid(p).wait_send()
        return carry

    lax.fori_loop(0, 3 * SUB, drain, 0)


def line_body(x, w, down, up, ids, store, slots):
    groups = lax.axis_size("replica")
    rows, depth = x.shape
    out_width = w.shape[1] // LINE
    width = out_width // SUB
    local_ranks = down.shape[1]
    needed = groups * WORKING_SLOTS
    picked_down, picked_up = pl.pallas_call(
        gather_kernel,
        out_shape=[
            jax.ShapeDtypeStruct((needed, local_ranks, down.shape[2]), BF16),
            jax.ShapeDtypeStruct((needed, local_ranks, up.shape[2]), BF16),
        ],
        in_specs=[SMEM, SMEM, ANY, ANY],
        out_specs=[ANY, ANY],
        scratch_shapes=[pltpu.SemaphoreType.DMA((2, needed))],
        name="gather",
    )(ids, store, down, up)
    shape = (groups, WORKING_SLOTS, local_ranks)
    picked_down = picked_down.reshape(shape + (down.shape[2],))
    picked_up = picked_up.reshape(shape + (up.shape[2],))
    dma = pltpu.SemaphoreType.DMA
    half = (rows // 2, 2 * ADAPTER_RANK)
    return pl.pallas_call(
        functools.partial(main_kernel, groups),
        out_shape=jax.ShapeDtypeStruct((rows, out_width), BF16),
        in_specs=[VMEM, VMEM, ANY, ANY, ANY],
        out_specs=VMEM,
        scratch_shapes=[
            pltpu.VMEM((SLOTS_W, depth, width), BF16),
            pltpu.VMEM((3 * SUB, rows, width), F32),
            pltpu.VMEM((3 * SUB, rows, width), BF16),
            pltpu.VMEM((3 * SUB, rows, width), BF16),
            pltpu.VMEM((SUB, rows, width), BF16),
            pltpu.VMEM((SUB, rows, width), BF16),
            pltpu.VMEM(picked_down.shape, BF16),
            pltpu.VMEM(picked_up.shape, BF16),
            pltpu.VMEM((needed * local_ranks, out_width), BF16),
            pltpu.VMEM(half, F32),
            pltpu.VMEM(half, F32),
            pltpu.VMEM(half, F32),
            pltpu.VMEM(half, F32),
            dma((SLOTS_W,)),
            dma((3 * SUB,)),
            dma((3 * SUB,)),
            dma((SUB,)),
            dma((SUB,)),
            dma((2, groups)),
            dma((2, groups)),
            dma((2,)),
            dma((3,)),
            dma((3,)),
        ],
        compiler_params=pltpu.CompilerParams(
            collective_id=0, has_side_effects=True, vmem_limit_bytes=56 * 1024 * 1024
        ),
        name="project",
    )(x, slots.reshape(rows, 1), w, picked_down, picked_up)


def solution(mesh):
    in_specs = (
        P("replica", "tensor"),
        P("tensor", None),
        P(None, "replica", "tensor"),
        P(None, "replica", "tensor"),
        P(),
        P(),
        P("replica"),
    )
    out_specs = P("replica", "tensor")
    on_line = mesh.shape["tensor"] == LINE and mesh.shape["replica"] * 8 == ADAPTER_RANK
    chosen = line_body if on_line else body
    return jax.shard_map(chosen, mesh=mesh, in_specs=in_specs, out_specs=out_specs, check_vma=False)
```

```python
import functools

import jax
import jax.numpy as jnp
from jax import lax
from jax.experimental import pallas as pl
from jax.experimental.pallas import tpu as pltpu
from jax.sharding import PartitionSpec as P

ADAPTER_RANK = 64
WORKING_SLOTS = 8


ADAPTER_SCALE = 0.5


def body(
    attention_heads_output,
    output_projection_weight,
    adapter_down_factors,
    adapter_up_factors,
    group_working_adapters,
    adapter_store_row,
    request_working_slot,
):
    groups = lax.axis_size("replica")
    row_count, features = attention_heads_output.shape
    local_rank_count = adapter_down_factors.shape[1]
    needed_store_rows = jnp.take(adapter_store_row, group_working_adapters.reshape(-1), axis=0)
    outgoing_down_factors = jnp.take(adapter_down_factors, needed_store_rows, axis=0)
    outgoing_up_factors = jnp.take(adapter_up_factors, needed_store_rows, axis=0)
    outgoing = jnp.stack([outgoing_down_factors, outgoing_up_factors], axis=1).reshape(
        groups, WORKING_SLOTS, 2, local_rank_count * features
    )
    fetched = lax.all_to_all(outgoing, "replica", split_axis=0, concat_axis=0, tiled=True)
    fetched = fetched.reshape(groups, WORKING_SLOTS, 2, local_rank_count, features).transpose(
        2, 1, 0, 3, 4
    )
    fetched = fetched.reshape(2, WORKING_SLOTS * ADAPTER_RANK, features)
    down_factor_rows = fetched[0]
    up_factor_rows = fetched[1]
    selector = (
        request_working_slot[:, None] == jnp.arange(WORKING_SLOTS, dtype=jnp.int32)[None, :]
    ).astype(jnp.float32)
    all_ranks = lax.dot_general(
        attention_heads_output,
        down_factor_rows,
        (((1,), (1,)), ((), ())),
        preferred_element_type=jnp.float32,
    )
    rank_local = jnp.sum(
        all_ranks.reshape(row_count, WORKING_SLOTS, ADAPTER_RANK) * selector[:, :, None], axis=1
    )
    base_local = jnp.dot(
        attention_heads_output, output_projection_weight, preferred_element_type=jnp.float32
    )
    base_projection_sum = lax.psum_scatter(base_local, "tensor", scatter_dimension=1, tiled=True)
    rank_total = lax.psum(rank_local, "tensor")
    rounded = rank_total.astype(jnp.bfloat16)
    expanded = (rounded[:, None, :] * selector[:, :, None].astype(jnp.bfloat16)).reshape(
        row_count, WORKING_SLOTS * ADAPTER_RANK
    )
    adapter_contribution = jnp.dot(expanded, up_factor_rows, preferred_element_type=jnp.float32)
    return (base_projection_sum + ADAPTER_SCALE * adapter_contribution).astype(jnp.bfloat16)


MESH = pl.DeviceIdType.MESH
ANY = pl.BlockSpec(memory_space=pl.ANY)
VMEM = pl.BlockSpec(memory_space=pltpu.VMEM)
SMEM = pl.BlockSpec(memory_space=pltpu.SMEM)
F32 = jnp.float32
BF16 = jnp.bfloat16

LINE = 4
SUB = 4
BLOCKS = LINE * SUB
WINDOW = 3
SLOTS_W = 4


def gather_kernel(ids, store, down, up, out_down, out_up, got, in_sems, out_sems):
    groups = out_down.shape[0]
    pairs = ((down, out_down), (up, out_up))

    def fetch(which, g, j, row):
        return pltpu.make_async_copy(
            pairs[which][0].at[row], got.at[which, g, j], in_sems.at[which, g * WORKING_SLOTS + j]
        )

    def put(which, g):
        return pltpu.make_async_copy(got.at[which, g], pairs[which][1].at[g], out_sems.at[which, g])

    for which in range(2):

        def start(g, carry):
            for j in range(WORKING_SLOTS):
                fetch(which, g, j, store[ids[g, j]]).start()
            return carry

        lax.fori_loop(0, groups, start, 0)
    for which in range(2):

        def forward(g, carry):
            for j in range(WORKING_SLOTS):
                fetch(which, g, j, 0).wait()
            put(which, g).start()
            return carry

        lax.fori_loop(0, groups, forward, 0)
    for which in range(2):

        def finish(g, carry):
            put(which, g).wait()
            return carry

        lax.fori_loop(0, groups, finish, 0)


def fold_matrix(columns, ranks, half):
    c = lax.broadcasted_iota(jnp.int32, (columns, 2 * ranks), 0)
    t = lax.broadcasted_iota(jnp.int32, (columns, 2 * ranks), 1)
    target = (c // (WORKING_SLOTS * 8)) * 8 + c % 8 + half * ranks
    return jnp.where(target == t, 1.0, 0.0).astype(BF16)


def spread_matrix(columns, ranks, half):
    t = lax.broadcasted_iota(jnp.int32, (2 * ranks, columns), 0)
    c = lax.broadcasted_iota(jnp.int32, (2 * ranks, columns), 1)
    target = (c // (WORKING_SLOTS * 8)) * 8 + c % 8 + half * ranks
    return jnp.where(target == t, 1.0, 0.0).astype(BF16)


def main_kernel(
    groups,
    x_ref, slot_ref, w_ref, down_ref, up_ref, out_ref,
    wbuf, acc, sbuf, from_end, from_mid, from_far, got_down, got_up, term,
    rank_own, rank_end, rank_far, rank_total,
    w_sem, send_sem, end_sem, mid_sem, far_sem, fetch_send, fetch_recv, own_sem, rank_send, rank_recv,
):
    me = lax.axis_index("replica")
    z = lax.axis_index("tensor")
    upper = z // 2
    inner = (z + upper) % 2
    is_end = inner == 0
    is_mid = inner == 1
    beside = 3 * upper + (1 - 2 * upper) * (1 - inner)
    far_mid = 3 * upper + (1 - 2 * upper) * 2
    far_end = 3 * upper + (1 - 2 * upper) * 3

    rows, depth = x_ref.shape
    width = out_ref.shape[1] // SUB
    ranks = ADAPTER_RANK
    fetched = groups * WORKING_SLOTS * 8

    def w_copy(p, slot):
        place = (3 + inner - p // SUB + LINE) % LINE
        chunk = 3 * upper + (1 - 2 * upper) * place
        column = pl.multiple_of((chunk * SUB + p % SUB) * width, width)
        return pltpu.make_async_copy(w_ref.at[:, pl.ds(column, width)], wbuf.at[slot], w_sem.at[slot])

    for p in range(SLOTS_W):
        w_copy(p, p).start()

    barrier = pltpu.get_barrier_semaphore()
    for k in range(1, groups):
        pl.semaphore_signal(barrier, inc=1, device_id=((me + k) % groups, z), device_id_type=MESH)
    for k in range(1, LINE):
        pl.semaphore_signal(barrier, inc=1, device_id=(me, (z + k) % LINE), device_id_type=MESH)
    pl.semaphore_wait(barrier, groups - 1 + LINE - 1)

    def fetch(which, k):
        src, dst = ((down_ref, got_down), (up_ref, got_up))[which]
        to = (me + k) % groups
        return pltpu.make_async_remote_copy(
            src_ref=src.at[to], dst_ref=dst.at[me],
            send_sem=fetch_send.at[which, k], recv_sem=fetch_recv.at[which, k],
            device_id=(to, z), device_id_type=MESH,
        )

    def fetch_own(which):
        src, dst = ((down_ref, got_down), (up_ref, got_up))[which]
        return pltpu.make_async_copy(src.at[me], dst.at[me], own_sem.at[which])

    def fetch_start(which):
        for k in range(1, groups):
            fetch(which, k).start()
        fetch_own(which).start()

    def fetch_wait(which):
        for k in range(1, groups):
            fetch(which, k).wait()
        fetch_own(which).wait()

    def to_beside_mid(p):
        return pltpu.make_async_remote_copy(
            src_ref=sbuf.at[p], dst_ref=from_end.at[p], send_sem=send_sem.at[p], recv_sem=end_sem.at[p],
            device_id=(me, beside), device_id_type=MESH)

    def to_beside_end(p):
        return pltpu.make_async_remote_copy(
            src_ref=sbuf.at[p], dst_ref=from_mid.at[p], send_sem=send_sem.at[p], recv_sem=mid_sem.at[p],
            device_id=(me, beside), device_id_type=MESH)

    def to_far(p, j, device):
        return pltpu.make_async_remote_copy(
            src_ref=sbuf.at[p], dst_ref=from_far.at[j], send_sem=send_sem.at[p], recv_sem=far_sem.at[j],
            device_id=(me, device), device_id_type=MESH)

    fetch_start(0)

    def block(p, carry):
        slot = p % SLOTS_W
        w_copy(p, slot).wait()
        part = jnp.dot(x_ref[...], wbuf[slot], preferred_element_type=F32)
        sent = jnp.where(is_end, p < 3 * SUB, p < SUB)

        @pl.when(sent)
        def _():
            sbuf[p] = part.astype(BF16)

        @pl.when(jnp.logical_not(sent))
        def _():
            acc[p - SUB] = part

        @pl.when(jnp.logical_and(is_end, p < WINDOW))
        def _():
            to_beside_mid(p).start()

        @pl.when(jnp.logical_and(is_mid, sent))
        def _():
            to_beside_end(p).start()

        @pl.when(p + SLOTS_W < BLOCKS)
        def _():
            w_copy(p + SLOTS_W, slot).start()

        return carry

    lax.fori_loop(0, BLOCKS, block, 0)

    def refill(p, carry):
        to_beside_mid(p - WINDOW).wait_send()
        to_beside_mid(p).start()
        return carry

    def merge(p, carry):
        to_beside_mid(p - SUB).wait_recv()
        sbuf[p] = (acc[p - SUB] + from_end[p - SUB].astype(F32)).astype(BF16)
        return carry

    def merge_far_end(j, carry):
        merge(SUB + j, carry)
        to_far(SUB + j, j, far_end).start()
        return carry

    def merge_far_mid(j, carry):
        merge(2 * SUB + j, carry)
        to_far(2 * SUB + j, j, far_mid).start()
        return carry

    @pl.when(is_end)
    def _():
        lax.fori_loop(WINDOW, 2 * WINDOW, refill, 0)

    @pl.when(is_mid)
    def _():
        lax.fori_loop(0, SUB, merge_far_end, 0)

    fetch_wait(0)
    fetch_start(1)
    down_rows = got_down[...].astype(F32).reshape(fetched, depth).astype(BF16)
    every = lax.dot_general(x_ref[...], down_rows, (((1,), (1,)), ((), ())), preferred_element_type=F32)
    column_slot = (lax.broadcasted_iota(jnp.int32, (rows, fetched), 1) // 8) % WORKING_SLOTS
    square = (rows, rows)
    diagonal = lax.broadcasted_iota(jnp.int32, square, 0) == lax.broadcasted_iota(jnp.int32, square, 1)
    slot = jnp.sum(jnp.where(diagonal, slot_ref[...].astype(F32), 0.0), axis=1, keepdims=True)
    chosen = slot == column_slot.astype(F32)
    every = jnp.where(chosen, every, 0.0)
    half = rows // 2
    total = jnp.zeros((half, 2 * ranks), F32)
    for h in range(2):
        rest = every[h * half:(h + 1) * half]
        matrix = fold_matrix(fetched, ranks, h)
        for _ in range(3):
            piece = rest.astype(BF16)
            total = total + jnp.dot(piece, matrix, preferred_element_type=F32)
            rest = rest - piece.astype(F32)
    rank_own[...] = total

    def rank_copy(i, src, dst, device):
        return pltpu.make_async_remote_copy(
            src_ref=src, dst_ref=dst, send_sem=rank_send.at[i], recv_sem=rank_recv.at[i],
            device_id=(me, device), device_id_type=MESH)

    to_mid = rank_copy(0, rank_own, rank_end, beside)
    across = rank_copy(1, rank_own, rank_far, far_mid)
    to_end = rank_copy(2, rank_own, rank_total, beside)

    @pl.when(is_end)
    def _():
        to_mid.start()
        lax.fori_loop(2 * WINDOW, 3 * SUB, refill, 0)

    @pl.when(is_mid)
    def _():
        to_mid.wait_recv()
        rank_own[...] += rank_end[...]
        across.start()
        across.wait_recv()
        across.wait_send()
        rank_own[...] += rank_far[...]
        to_end.start()
        rank_total[...] = rank_own[...]
        lax.fori_loop(0, SUB, merge_far_mid, 0)
        to_end.wait_send()

    @pl.when(is_end)
    def _():
        to_mid.wait_send()
        to_end.wait_recv()

    fetch_wait(1)
    rounded = rank_total[...].astype(BF16)
    parts = [
        jnp.dot(rounded, spread_matrix(fetched, ranks, h), preferred_element_type=F32) for h in range(2)
    ]
    expanded = jnp.where(chosen, jnp.concatenate(parts, axis=0), 0.0).astype(BF16)
    term[...] = got_up[...].astype(F32).reshape(fetched, out_ref.shape[1]).astype(BF16)

    for j in range(SUB):
        columns = slice(j * width, (j + 1) * width)
        adapter = jnp.dot(expanded, term[:, columns], preferred_element_type=F32)
        acc[2 * SUB + j] += ADAPTER_SCALE * adapter

    for j in range(SUB):
        columns = slice(j * width, (j + 1) * width)
        to_far(j, j, far_mid).wait_recv()

        @pl.when(is_end)
        def _():
            to_beside_end(j).wait_recv()
            total = acc[2 * SUB + j] + from_mid[j].astype(F32) + from_far[j].astype(F32)
            out_ref[:, columns] = total.astype(BF16)

        @pl.when(is_mid)
        def _():
            to_beside_mid(2 * SUB + j).wait_recv()
            total = acc[2 * SUB + j] + from_end[2 * SUB + j].astype(F32) + from_far[j].astype(F32)
            out_ref[:, columns] = total.astype(BF16)

    def drain(p, carry):
        to_beside_mid(p).wait_send()
        return carry

    @pl.when(is_mid)
    def _():
        lax.fori_loop(0, 3 * SUB - WINDOW, drain, 0)

    lax.fori_loop(3 * SUB - WINDOW, 3 * SUB, drain, 0)


def line_body(x, w, down, up, ids, store, slots):
    groups = lax.axis_size("replica")
    rows, depth = x.shape
    out_width = w.shape[1] // LINE
    width = out_width // SUB
    local_ranks = down.shape[1]
    needed = groups * WORKING_SLOTS
    shape = (groups, WORKING_SLOTS, local_ranks)
    picked_down, picked_up = pl.pallas_call(
        gather_kernel,
        out_shape=[
            jax.ShapeDtypeStruct(shape + (down.shape[2],), BF16),
            jax.ShapeDtypeStruct(shape + (up.shape[2],), BF16),
        ],
        in_specs=[SMEM, SMEM, ANY, ANY],
        out_specs=[ANY, ANY],
        scratch_shapes=[
            pltpu.VMEM((2,) + shape + (depth,), BF16),
            pltpu.SemaphoreType.DMA((2, needed)),
            pltpu.SemaphoreType.DMA((2, groups)),
        ],
        compiler_params=pltpu.CompilerParams(vmem_limit_bytes=56 * 1024 * 1024),
        name="gather",
    )(ids, store, down, up)
    dma = pltpu.SemaphoreType.DMA
    half = (rows // 2, 2 * ADAPTER_RANK)
    return pl.pallas_call(
        functools.partial(main_kernel, groups),
        out_shape=jax.ShapeDtypeStruct((rows, out_width), BF16),
        in_specs=[VMEM, VMEM, ANY, ANY, ANY],
        out_specs=VMEM,
        scratch_shapes=[
            pltpu.VMEM((SLOTS_W, depth, width), BF16),
            pltpu.VMEM((3 * SUB, rows, width), F32),
            pltpu.VMEM((3 * SUB, rows, width), BF16),
            pltpu.VMEM((3 * SUB, rows, width), BF16),
            pltpu.VMEM((SUB, rows, width), BF16),
            pltpu.VMEM((SUB, rows, width), BF16),
            pltpu.VMEM(picked_down.shape, BF16),
            pltpu.VMEM(picked_up.shape, BF16),
            pltpu.VMEM((needed * local_ranks, out_width), BF16),
            pltpu.VMEM(half, F32),
            pltpu.VMEM(half, F32),
            pltpu.VMEM(half, F32),
            pltpu.VMEM(half, F32),
            dma((SLOTS_W,)),
            dma((3 * SUB,)),
            dma((3 * SUB,)),
            dma((SUB,)),
            dma((SUB,)),
            dma((2, groups)),
            dma((2, groups)),
            dma((2,)),
            dma((3,)),
            dma((3,)),
        ],
        compiler_params=pltpu.CompilerParams(
            collective_id=0, has_side_effects=True, vmem_limit_bytes=56 * 1024 * 1024
        ),
        name="project",
    )(x, slots.reshape(1, rows), w, picked_down, picked_up)


def solution(mesh):
    in_specs = (
        P("replica", "tensor"),
        P("tensor", None),
        P(None, "replica", "tensor"),
        P(None, "replica", "tensor"),
        P(),
        P(),
        P("replica"),
    )
    out_specs = P("replica", "tensor")
    on_line = mesh.shape["tensor"] == LINE and mesh.shape["replica"] * 8 == ADAPTER_RANK
    chosen = line_body if on_line else body
    return jax.shard_map(chosen, mesh=mesh, in_specs=in_specs, out_specs=out_specs, check_vma=False)
```

```python
import functools

import jax
import jax.numpy as jnp
from jax import lax
from jax.experimental import pallas as pl
from jax.experimental.pallas import tpu as pltpu
from jax.sharding import PartitionSpec as P

ADAPTER_RANK = 64
WORKING_SLOTS = 8


ADAPTER_SCALE = 0.5


def body(
    attention_heads_output,
    output_projection_weight,
    adapter_down_factors,
    adapter_up_factors,
    group_working_adapters,
    adapter_store_row,
    request_working_slot,
):
    groups = lax.axis_size("replica")
    row_count, features = attention_heads_output.shape
    local_rank_count = adapter_down_factors.shape[1]
    needed_store_rows = jnp.take(adapter_store_row, group_working_adapters.reshape(-1), axis=0)
    outgoing_down_factors = jnp.take(adapter_down_factors, needed_store_rows, axis=0)
    outgoing_up_factors = jnp.take(adapter_up_factors, needed_store_rows, axis=0)
    outgoing = jnp.stack([outgoing_down_factors, outgoing_up_factors], axis=1).reshape(
        groups, WORKING_SLOTS, 2, local_rank_count * features
    )
    fetched = lax.all_to_all(outgoing, "replica", split_axis=0, concat_axis=0, tiled=True)
    fetched = fetched.reshape(groups, WORKING_SLOTS, 2, local_rank_count, features).transpose(
        2, 1, 0, 3, 4
    )
    fetched = fetched.reshape(2, WORKING_SLOTS * ADAPTER_RANK, features)
    down_factor_rows = fetched[0]
    up_factor_rows = fetched[1]
    selector = (
        request_working_slot[:, None] == jnp.arange(WORKING_SLOTS, dtype=jnp.int32)[None, :]
    ).astype(jnp.float32)
    all_ranks = lax.dot_general(
        attention_heads_output,
        down_factor_rows,
        (((1,), (1,)), ((), ())),
        preferred_element_type=jnp.float32,
    )
    rank_local = jnp.sum(
        all_ranks.reshape(row_count, WORKING_SLOTS, ADAPTER_RANK) * selector[:, :, None], axis=1
    )
    base_local = jnp.dot(
        attention_heads_output, output_projection_weight, preferred_element_type=jnp.float32
    )
    base_projection_sum = lax.psum_scatter(base_local, "tensor", scatter_dimension=1, tiled=True)
    rank_total = lax.psum(rank_local, "tensor")
    rounded = rank_total.astype(jnp.bfloat16)
    expanded = (rounded[:, None, :] * selector[:, :, None].astype(jnp.bfloat16)).reshape(
        row_count, WORKING_SLOTS * ADAPTER_RANK
    )
    adapter_contribution = jnp.dot(expanded, up_factor_rows, preferred_element_type=jnp.float32)
    return (base_projection_sum + ADAPTER_SCALE * adapter_contribution).astype(jnp.bfloat16)


MESH = pl.DeviceIdType.MESH
ANY = pl.BlockSpec(memory_space=pl.ANY)
VMEM = pl.BlockSpec(memory_space=pltpu.VMEM)
SMEM = pl.BlockSpec(memory_space=pltpu.SMEM)
F32 = jnp.float32
BF16 = jnp.bfloat16

LINE = 4
SUB = 4
BLOCKS = LINE * SUB
WINDOW = 3
EARLY = 7
SLOTS_W = 4


def gather_kernel(ids, store, down, up, out_down, out_up, got, in_sems, out_sems):
    groups = out_down.shape[0]
    pairs = ((down, out_down), (up, out_up))

    def fetch(which, g, j, row):
        return pltpu.make_async_copy(
            pairs[which][0].at[row], got.at[which, g, j], in_sems.at[which, g * WORKING_SLOTS + j]
        )

    def put(which, g):
        return pltpu.make_async_copy(got.at[which, g], pairs[which][1].at[g], out_sems.at[which, g])

    for which in range(2):

        def start(g, carry):
            for j in range(WORKING_SLOTS):
                fetch(which, g, j, store[ids[g, j]]).start()
            return carry

        lax.fori_loop(0, groups, start, 0)
    for which in range(2):

        def forward(g, carry):
            for j in range(WORKING_SLOTS):
                fetch(which, g, j, 0).wait()
            put(which, g).start()
            return carry

        lax.fori_loop(0, groups, forward, 0)
    for which in range(2):

        def finish(g, carry):
            put(which, g).wait()
            return carry

        lax.fori_loop(0, groups, finish, 0)


def fold_matrix(columns, ranks, half):
    c = lax.broadcasted_iota(jnp.int32, (columns, 2 * ranks), 0)
    t = lax.broadcasted_iota(jnp.int32, (columns, 2 * ranks), 1)
    target = (c // (WORKING_SLOTS * 8)) * 8 + c % 8 + half * ranks
    return jnp.where(target == t, 1.0, 0.0).astype(BF16)


def spread_matrix(columns, ranks, half):
    t = lax.broadcasted_iota(jnp.int32, (2 * ranks, columns), 0)
    c = lax.broadcasted_iota(jnp.int32, (2 * ranks, columns), 1)
    target = (c // (WORKING_SLOTS * 8)) * 8 + c % 8 + half * ranks
    return jnp.where(target == t, 1.0, 0.0).astype(BF16)


def main_kernel(
    groups,
    x_ref, slot_ref, w_ref, down_ref, up_ref, out_ref,
    wbuf, acc, sbuf, from_end, from_mid, from_far, got_down, got_up, term,
    rank_own, rank_end, rank_far, rank_total,
    w_sem, send_sem, end_sem, mid_sem, far_sem, fetch_send, fetch_recv, own_sem, rank_send, rank_recv,
):
    me = lax.axis_index("replica")
    z = lax.axis_index("tensor")
    upper = z // 2
    inner = (z + upper) % 2
    is_end = inner == 0
    is_mid = inner == 1
    beside = 3 * upper + (1 - 2 * upper) * (1 - inner)
    far_mid = 3 * upper + (1 - 2 * upper) * 2
    far_end = 3 * upper + (1 - 2 * upper) * 3

    rows, depth = x_ref.shape
    width = out_ref.shape[1] // SUB
    ranks = ADAPTER_RANK
    fetched = groups * WORKING_SLOTS * 8

    def w_copy(p, slot):
        place = (3 + inner - p // SUB + LINE) % LINE
        chunk = 3 * upper + (1 - 2 * upper) * place
        column = pl.multiple_of((chunk * SUB + p % SUB) * width, width)
        return pltpu.make_async_copy(w_ref.at[:, pl.ds(column, width)], wbuf.at[slot], w_sem.at[slot])

    for p in range(SLOTS_W):
        w_copy(p, p).start()

    barrier = pltpu.get_barrier_semaphore()
    for k in range(1, groups):
        pl.semaphore_signal(barrier, inc=1, device_id=((me + k) % groups, z), device_id_type=MESH)
    for k in range(1, LINE):
        pl.semaphore_signal(barrier, inc=1, device_id=(me, (z + k) % LINE), device_id_type=MESH)
    pl.semaphore_wait(barrier, groups - 1 + LINE - 1)

    def fetch(which, k):
        src, dst = ((down_ref, got_down), (up_ref, got_up))[which]
        to = (me + k) % groups
        return pltpu.make_async_remote_copy(
            src_ref=src.at[to], dst_ref=dst.at[me],
            send_sem=fetch_send.at[which, k], recv_sem=fetch_recv.at[which, k],
            device_id=(to, z), device_id_type=MESH,
        )

    def fetch_own(which):
        src, dst = ((down_ref, got_down), (up_ref, got_up))[which]
        return pltpu.make_async_copy(src.at[me], dst.at[me], own_sem.at[which])

    def fetch_start(which):
        for k in range(1, groups):
            fetch(which, k).start()
        fetch_own(which).start()

    def fetch_wait(which):
        for k in range(1, groups):
            fetch(which, k).wait()
        fetch_own(which).wait()

    def to_beside_mid(p):
        return pltpu.make_async_remote_copy(
            src_ref=sbuf.at[p], dst_ref=from_end.at[p], send_sem=send_sem.at[p], recv_sem=end_sem.at[p],
            device_id=(me, beside), device_id_type=MESH)

    def to_beside_end(p):
        return pltpu.make_async_remote_copy(
            src_ref=sbuf.at[p], dst_ref=from_mid.at[p], send_sem=send_sem.at[p], recv_sem=mid_sem.at[p],
            device_id=(me, beside), device_id_type=MESH)

    def to_far(p, j, device):
        return pltpu.make_async_remote_copy(
            src_ref=sbuf.at[p], dst_ref=from_far.at[j], send_sem=send_sem.at[p], recv_sem=far_sem.at[j],
            device_id=(me, device), device_id_type=MESH)

    fetch_start(0)

    def block(p, carry):
        slot = p % SLOTS_W
        w_copy(p, slot).wait()
        part = jnp.dot(x_ref[...], wbuf[slot], preferred_element_type=F32)
        sent = jnp.where(is_end, p < 3 * SUB, p < SUB)

        @pl.when(sent)
        def _():
            sbuf[p] = part.astype(BF16)

        @pl.when(jnp.logical_not(sent))
        def _():
            acc[p - SUB] = part

        @pl.when(jnp.logical_and(is_end, p < WINDOW))
        def _():
            to_beside_mid(p).start()

        @pl.when(jnp.logical_and(is_mid, sent))
        def _():
            to_beside_end(p).start()

        @pl.when(p + SLOTS_W < BLOCKS)
        def _():
            w_copy(p + SLOTS_W, slot).start()

        return carry

    lax.fori_loop(0, BLOCKS, block, 0)

    def refill(p, carry):
        to_beside_mid(p - WINDOW).wait_send()
        to_beside_mid(p).start()
        return carry

    def merge(p, carry):
        to_beside_mid(p - SUB).wait_recv()
        sbuf[p] = (acc[p - SUB] + from_end[p - SUB].astype(F32)).astype(BF16)
        return carry

    def merge_far_end(j, carry):
        merge(SUB + j, carry)
        to_far(SUB + j, j, far_end).start()
        return carry

    def merge_far_mid(j, carry):
        merge(2 * SUB + j, carry)
        to_far(2 * SUB + j, j, far_mid).start()
        return carry

    @pl.when(is_end)
    def _():
        lax.fori_loop(WINDOW, EARLY, refill, 0)

    @pl.when(is_mid)
    def _():
        lax.fori_loop(0, SUB, merge_far_end, 0)

    fetch_wait(0)
    fetch_start(1)
    down_rows = got_down[...].astype(F32).reshape(fetched, depth).astype(BF16)
    every = lax.dot_general(x_ref[...], down_rows, (((1,), (1,)), ((), ())), preferred_element_type=F32)
    column_slot = (lax.broadcasted_iota(jnp.int32, (rows, fetched), 1) // 8) % WORKING_SLOTS
    square = (rows, rows)
    diagonal = lax.broadcasted_iota(jnp.int32, square, 0) == lax.broadcasted_iota(jnp.int32, square, 1)
    slot = jnp.sum(jnp.where(diagonal, slot_ref[...].astype(F32), 0.0), axis=1, keepdims=True)
    chosen = slot == column_slot.astype(F32)
    every = jnp.where(chosen, every, 0.0)
    half = rows // 2
    total = jnp.zeros((half, 2 * ranks), F32)
    for h in range(2):
        rest = every[h * half:(h + 1) * half]
        matrix = fold_matrix(fetched, ranks, h)
        for _ in range(3):
            piece = rest.astype(BF16)
            total = total + jnp.dot(piece, matrix, preferred_element_type=F32)
            rest = rest - piece.astype(F32)
    rank_own[...] = total

    def rank_copy(i, src, dst, device):
        return pltpu.make_async_remote_copy(
            src_ref=src, dst_ref=dst, send_sem=rank_send.at[i], recv_sem=rank_recv.at[i],
            device_id=(me, device), device_id_type=MESH)

    to_mid = rank_copy(0, rank_own, rank_end, beside)
    across = rank_copy(1, rank_own, rank_far, far_mid)
    to_end = rank_copy(2, rank_own, rank_total, beside)

    @pl.when(is_end)
    def _():
        to_mid.start()
        lax.fori_loop(EARLY, 3 * SUB, refill, 0)

    @pl.when(is_mid)
    def _():
        lax.fori_loop(0, SUB, merge_far_mid, 0)
        to_mid.wait_recv()
        rank_own[...] += rank_end[...]
        across.start()

    fetch_wait(1)
    term[...] = got_up[...].astype(F32).reshape(fetched, out_ref.shape[1]).astype(BF16)

    @pl.when(is_mid)
    def _():
        across.wait_recv()
        across.wait_send()
        rank_own[...] += rank_far[...]
        to_end.start()
        rank_total[...] = rank_own[...]

    @pl.when(is_end)
    def _():
        to_mid.wait_send()
        to_end.wait_recv()

    rounded = rank_total[...].astype(BF16)
    parts = [
        jnp.dot(rounded, spread_matrix(fetched, ranks, h), preferred_element_type=F32) for h in range(2)
    ]
    expanded = jnp.where(chosen, jnp.concatenate(parts, axis=0), 0.0).astype(BF16)

    for j in range(SUB):
        columns = slice(j * width, (j + 1) * width)
        adapter = jnp.dot(expanded, term[:, columns], preferred_element_type=F32)
        acc[2 * SUB + j] += ADAPTER_SCALE * adapter

    for j in range(SUB):
        columns = slice(j * width, (j + 1) * width)
        to_far(j, j, far_mid).wait_recv()

        @pl.when(is_end)
        def _():
            to_beside_end(j).wait_recv()
            total = acc[2 * SUB + j] + from_mid[j].astype(F32) + from_far[j].astype(F32)
            out_ref[:, columns] = total.astype(BF16)

        @pl.when(is_mid)
        def _():
            to_beside_mid(2 * SUB + j).wait_recv()
            total = acc[2 * SUB + j] + from_end[2 * SUB + j].astype(F32) + from_far[j].astype(F32)
            out_ref[:, columns] = total.astype(BF16)

    def drain(p, carry):
        to_beside_mid(p).wait_send()
        return carry

    @pl.when(is_mid)
    def _():
        to_end.wait_send()
        lax.fori_loop(0, 3 * SUB - WINDOW, drain, 0)

    lax.fori_loop(3 * SUB - WINDOW, 3 * SUB, drain, 0)


def line_body(x, w, down, up, ids, store, slots):
    groups = lax.axis_size("replica")
    rows, depth = x.shape
    out_width = w.shape[1] // LINE
    width = out_width // SUB
    local_ranks = down.shape[1]
    needed = groups * WORKING_SLOTS
    shape = (groups, WORKING_SLOTS, local_ranks)
    picked_down, picked_up = pl.pallas_call(
        gather_kernel,
        out_shape=[
            jax.ShapeDtypeStruct(shape + (down.shape[2],), BF16),
            jax.ShapeDtypeStruct(shape + (up.shape[2],), BF16),
        ],
        in_specs=[SMEM, SMEM, ANY, ANY],
        out_specs=[ANY, ANY],
        scratch_shapes=[
            pltpu.VMEM((2,) + shape + (depth,), BF16),
            pltpu.SemaphoreType.DMA((2, needed)),
            pltpu.SemaphoreType.DMA((2, groups)),
        ],
        compiler_params=pltpu.CompilerParams(vmem_limit_bytes=56 * 1024 * 1024),
        name="gather",
    )(ids, store, down, up)
    dma = pltpu.SemaphoreType.DMA
    half = (rows // 2, 2 * ADAPTER_RANK)
    return pl.pallas_call(
        functools.partial(main_kernel, groups),
        out_shape=jax.ShapeDtypeStruct((rows, out_width), BF16),
        in_specs=[VMEM, VMEM, ANY, ANY, ANY],
        out_specs=VMEM,
        scratch_shapes=[
            pltpu.VMEM((SLOTS_W, depth, width), BF16),
            pltpu.VMEM((3 * SUB, rows, width), F32),
            pltpu.VMEM((3 * SUB, rows, width), BF16),
            pltpu.VMEM((3 * SUB, rows, width), BF16),
            pltpu.VMEM((SUB, rows, width), BF16),
            pltpu.VMEM((SUB, rows, width), BF16),
            pltpu.VMEM(picked_down.shape, BF16),
            pltpu.VMEM(picked_up.shape, BF16),
            pltpu.VMEM((needed * local_ranks, out_width), BF16),
            pltpu.VMEM(half, F32),
            pltpu.VMEM(half, F32),
            pltpu.VMEM(half, F32),
            pltpu.VMEM(half, F32),
            dma((SLOTS_W,)),
            dma((3 * SUB,)),
            dma((3 * SUB,)),
            dma((SUB,)),
            dma((SUB,)),
            dma((2, groups)),
            dma((2, groups)),
            dma((2,)),
            dma((3,)),
            dma((3,)),
        ],
        compiler_params=pltpu.CompilerParams(
            collective_id=0, has_side_effects=True, vmem_limit_bytes=56 * 1024 * 1024
        ),
        name="project",
    )(x, slots.reshape(1, rows), w, picked_down, picked_up)


def solution(mesh):
    in_specs = (
        P("replica", "tensor"),
        P("tensor", None),
        P(None, "replica", "tensor"),
        P(None, "replica", "tensor"),
        P(),
        P(),
        P("replica"),
    )
    out_specs = P("replica", "tensor")
    on_line = mesh.shape["tensor"] == LINE and mesh.shape["replica"] * 8 == ADAPTER_RANK
    chosen = line_body if on_line else body
    return jax.shard_map(chosen, mesh=mesh, in_specs=in_specs, out_specs=out_specs, check_vma=False)
```
